256 devices in a mesh: sta: 32 (over z, y), freq: 8 (over x, core).
Axes of the slice: x: 4, y: 4, z: 8, core: 2. Of those that a mesh axis runs over, the one named last changes fastest.
Arguments:
- spectra: bfloat16 [8, 2048, 2, 4096], P(None, 'sta', None, 'freq'), may hold values from -6 to 6
- pair_blocks: int32 [32, 2], P('sta'), may hold values from 0 to 31, as said below
Outputs:
- correlations: float32 [64, 32, 64, 1024], P('freq', 'sta')
The draws below stay inside these ranges and needn't reach their ends.
Inputs may be any that keep to these rules, and one draw needn't show every extreme that they name: `pair_blocks`: in every row the first block is smaller than the second, and both lie within 4 blocks of the row's owner p; the first row of each owner pairs the lowest and the highest block of that range.
All inputs are finite; a program needn't handle non-finite values.
Results may differ from the reference program's by a relative error of at most 0.0037.
Values may be sent and summed in bfloat16 or wider, within the bound.
A program may use at most 128 MiB of HBM per device.

```python
import math
import jax
import jax.numpy as jnp
from jax import lax

BLK = 64
NBIN = 4096
LAGS = 1024
WIN = 8
PB_DEV = 1
REACH = 4
NBLOCK = 32
STATIONS = 2048
NPAIR = 32


def draw_pair_blocks(key, part):
    key = jax.random.fold_in(key, 7)
    key_first, key_second = jax.random.split(key)
    row_index = lax.iota(jnp.int32, NPAIR)
    owner_index = row_index // PB_DEV
    slot_index = row_index % PB_DEV
    lowest = jnp.maximum(owner_index - REACH, 0)
    highest = jnp.minimum(owner_index + REACH, NBLOCK - 1)
    first_slot = jax.random.randint(key_first, (NPAIR,), lowest, highest)
    second_slot = jax.random.randint(key_second, (NPAIR,), first_slot + 1, highest + 1)
    first_slot = jnp.where(slot_index == 0, lowest, first_slot)
    second_slot = jnp.where(slot_index == 0, highest, second_slot)
    return jnp.stack([first_slot, second_slot], axis=1).astype(jnp.int32)


def shard_levels(stream_key, extent, pieces, smallest, top_value):
    def one(dim, blocks):
        heights = jax.random.uniform(jax.random.fold_in(jax.random.fold_in(stream_key, 6), dim), (blocks,), jnp.float32, smallest / len(pieces), top_value / len(pieces))
        return jnp.repeat(jnp.exp(heights), extent[dim] // blocks).reshape((-1,) + (1,) * (len(extent) - dim - 1))

    factor_of = one(*pieces[0])
    for cut in pieces[1:]:
        factor_of = factor_of * one(*cut)
    return factor_of


def bell_draw(rng, extent, width, limit, pieces=(), kind=jnp.bfloat16):
    factor_of = shard_levels(rng, extent, pieces, -0.22, 0.18) if pieces else 1.0
    entries = jax.random.normal(rng, extent, jnp.float32) * width * factor_of
    return jnp.minimum(jnp.maximum(entries, -limit), limit).astype(kind)


def setup_inputs(seed: int = 0) -> dict:
    seeds = jax.random.split(jax.random.key(seed), 3)
    return {
        "spectra": bell_draw(seeds[0], (WIN, STATIONS, 2, NBIN), 1.0, 6.0, ((1, 32), (3, 8))),
        "pair_blocks": draw_pair_blocks(jax.random.fold_in(seeds[2], 71), 0),
    }


def table_rows(row_start, bin_count, lag_count, fft_length):
    bin_index = row_start + lax.iota(jnp.int32, bin_count)
    lag_offset = lax.iota(jnp.int32, lag_count) - lag_count // 2
    phase_index = bin_index[:, None] * lag_offset[None, :] % fft_length
    angles = phase_index.astype(jnp.float32) * (2.0 * math.pi / fft_length)
    return jnp.concatenate([jnp.cos(angles), -jnp.sin(angles)], 0).astype(jnp.bfloat16)

def reference(spectra, pair_blocks):
    dft_table = table_rows(0, NBIN, LAGS, 2 * NBIN)
    norm_factor = 1.0 / math.sqrt(WIN * NBIN)

    def pair_block_corr(pair_row):
        left_blocks = lax.dynamic_slice_in_dim(spectra, (pair_row[0] * BLK).astype(jnp.int32), BLK, 1).astype(jnp.float32)
        right_blocks = lax.dynamic_slice_in_dim(spectra, (pair_row[1] * BLK).astype(jnp.int32), BLK, 1).astype(jnp.float32)
        turned = jnp.stack([-right_blocks[:, :, 1], right_blocks[:, :, 0]], axis=2)
        real_part = jnp.einsum('wacf,wbcf->abf', left_blocks, right_blocks)
        imag_part = jnp.einsum('wacf,wbcf->abf', left_blocks, turned)
        cross_spec = jnp.stack([real_part, imag_part], axis=2).astype(jnp.bfloat16)
        flat_rows = cross_spec.reshape(BLK * BLK, 2 * NBIN)
        summed = jnp.dot(flat_rows, dft_table, preferred_element_type=jnp.float32)
        return (summed * norm_factor).reshape(BLK, BLK, LAGS)
    stacked = lax.map(pair_block_corr, pair_blocks)
    return jnp.transpose(stacked, (1, 0, 2, 3))
```

```python
import functools
import math

import jax
import jax.numpy as jnp
import ml_dtypes
import numpy as np
from jax import lax
from jax.experimental import pallas as pl
from jax.experimental.pallas import tpu as pltpu
from jax.sharding import PartitionSpec as P

LAGS = 1024
WIN = 8
BLK = 64
NY = 4
LANES = 128
MESH = pl.DeviceIdType.MESH
F32 = jnp.float32
BF16 = jnp.bfloat16

SOURCES = ((0, 0), (0, 1), (1, 0), (3, 0), (1, 1), (3, 1), (2, 0), (2, 1))


def table_pieces(parts, steps, bins_total):
    fft_length = 2 * bins_total
    bins = np.arange(bins_total, dtype=np.int64)
    lags = np.arange(LAGS, dtype=np.int64) - LAGS // 2
    angles = ((bins[:, None] * lags[None, :]) % fft_length) * (2.0 * math.pi / fft_length)
    both = np.stack([np.cos(angles), -np.sin(angles)]).astype(np.float32)
    both = both.reshape(2, parts, steps, LANES, LAGS).transpose(1, 2, 0, 3, 4)
    return both.reshape(parts, steps, 2 * LANES, LAGS).astype(ml_dtypes.bfloat16)


def kernel(rows_z, steps, norm, s_ref, t_ref, o_ref, y_buf, x_in, x_buf, table, lhs, xf,
           xz_sem, yz_sem, y_sem, x_sem, t_sem, xo_sem, yo_sem, xe_sem, ye_sem, ys_sem, xs_sem):
    sta = lax.axis_index("sta")
    me = lax.axis_index("freq")
    z = sta // NY
    yy = sta % NY
    chip = me // 2
    core = me % 2
    last = rows_z * NY - 1
    up = (me + 2) % 8
    down = (me + 6) % 8
    mate = me + 1 - 2 * core

    def peer(dr, ds):
        return 2 * ((chip + dr) % 4) + (core + ds) % 2

    x_low = z == 0
    y_high = z == rows_z - 1
    x_src = sta == 0
    y_src = sta == last
    x_pass = jnp.logical_and(x_low, yy % 2 == 1)
    y_pass = jnp.logical_and(y_high, yy % 2 == 0)
    x_half = jnp.where(yy == 1, 0, 4)
    y_half = jnp.where(yy == 2, 0, 4)

    barrier = pltpu.get_barrier_semaphore()

    def greet(row, col):
        pl.semaphore_signal(barrier, inc=1, device_id=(row, col), device_id_type=MESH)

    for dr, ds in SOURCES[1:]:
        greet(sta, peer(dr, ds))

    @pl.when(z > 0)
    def _():
        greet(sta - NY, me)

    @pl.when(z < rows_z - 1)
    def _():
        greet(sta + NY, me)

    @pl.when(x_pass)
    def _():
        greet(0, me)

    @pl.when(jnp.logical_and(x_low, yy == 2))
    def _():
        greet(1, me)
        greet(3, me)

    @pl.when(y_pass)
    def _():
        greet(last, me)

    @pl.when(jnp.logical_and(y_high, yy == 1))
    def _():
        greet(last - 1, me)
        greet(last - 3, me)

    expected = 7
    for flag, count in ((z < rows_z - 1, 1), (z > 0, 1), (x_src, 2), (y_src, 2), (x_pass, 1), (y_pass, 1)):
        expected = expected + jnp.where(flag, count, 0)
    pl.semaphore_wait(barrier, expected)

    def remote(src, dst, send, recv, row, col):
        return pltpu.make_async_remote_copy(
            src_ref=src, dst_ref=dst, send_sem=send, recv_sem=recv,
            device_id=(row, col), device_id_type=MESH)

    def x_out(t):
        return remote(s_ref.at[t], x_in.at[t], xo_sem.at[t], xz_sem.at[t], sta + NY, me)

    def y_out(t):
        return remote(s_ref.at[t], y_buf.at[0, 0, t], yo_sem.at[t], yz_sem.at[t], sta - NY, me)

    def x_edge(t, n):
        return remote(s_ref.at[t], x_in.at[t], xe_sem.at[t, n], xz_sem.at[t], 1 + 2 * n, me)

    def y_edge(t, n):
        return remote(s_ref.at[t], y_buf.at[0, 0, t], ye_sem.at[t, n], yz_sem.at[t], last - 1 - 2 * n, me)

    def x_own(t):
        return pltpu.make_async_copy(s_ref.at[t], x_in.at[t], xz_sem.at[t])

    def y_own(t):
        return pltpu.make_async_copy(s_ref.at[t], y_buf.at[0, 0, t], yz_sem.at[t])

    def x_relay(t):
        piece = x_in.at[t, pl.ds(x_half, 4)]
        return remote(piece, piece, xe_sem.at[t, 0], xz_sem.at[t], 2, me)

    def y_relay(t):
        piece = y_buf.at[0, 0, t, pl.ds(y_half, 4)]
        return remote(piece, piece, ye_sem.at[t, 0], yz_sem.at[t], last - 2, me)

    def y_copy(t, n, src, dst, col, lo=0, size=8):
        return remote(y_buf.at[src[0], src[1], t, pl.ds(lo, size)], y_buf.at[dst[0], dst[1], t, pl.ds(lo, size)],
                      ys_sem.at[t, n], y_sem.at[dst[0], dst[1], t], sta, col)

    def y_first(t):
        return (y_copy(t, 0, (0, 0), (3, 0), up), y_copy(t, 1, (0, 0), (1, 0), down),
                y_copy(t, 2, (0, 0), (0, 1), mate))

    def y_second(t):
        return (y_copy(t, 3, (3, 0), (2, 0), up, 0, 4), y_copy(t, 4, (3, 0), (3, 1), mate),
                y_copy(t, 5, (1, 0), (2, 0), down, 4, 4), y_copy(t, 6, (1, 0), (1, 1), mate))

    def y_third(t):
        return (y_copy(t, 7, (2, 0), (2, 1), mate),)

    def x_copies(t):
        return [
            remote(x_in.at[t, peer(dr, ds)], x_buf.at[(4 - dr) % 4, ds, t], xs_sem.at[t, n],
                   x_sem.at[(4 - dr) % 4, ds, t], sta, peer(dr, ds))
            for n, (dr, ds) in enumerate(SOURCES) if n]

    def x_mine(t):
        return pltpu.make_async_copy(x_in.at[t, me], x_buf.at[0, 0, t], x_sem.at[0, 0, t])

    def arrived(ref, sem):
        pltpu.make_async_copy(ref, ref, sem).wait()

    def table_copy(t, n):
        dr, ds = SOURCES[n]
        return pltpu.make_async_copy(t_ref.at[peer(dr, ds), t], table.at[t, pl.ds(2 * LANES * n, 2 * LANES)],
                                     t_sem.at[t, n])

    def each_start(t, start):
        def go(copy):
            if start:
                copy.start()
            else:
                copy.wait_send()

        @pl.when(z < rows_z - 1)
        def _():
            go(x_out(t))

        @pl.when(z > 0)
        def _():
            go(y_out(t))

        @pl.when(x_src)
        def _():
            go(x_edge(t, 0))
            go(x_edge(t, 1))
            if start:
                x_own(t).start()

        @pl.when(y_src)
        def _():
            go(y_edge(t, 0))
            go(y_edge(t, 1))
            if start:
                y_own(t).start()

    def enter(t):
        arrived(y_buf.at[0, 0, t], yz_sem.at[t])
        for copy in y_first(t):
            copy.start()

        @pl.when(y_pass)
        def _():
            y_relay(t).start()

        arrived(x_in.at[t], xz_sem.at[t])
        x_mine(t).start()
        for copy in x_copies(t):
            copy.start()

        @pl.when(x_pass)
        def _():
            x_relay(t).start()

    def cross(t, n):
        r, s = SOURCES[n]
        arrived(x_buf.at[r, s, t], x_sem.at[r, s, t])
        xf[...] = x_buf[r, s, t].astype(F32)

        def body(j, carry):
            pair = []
            for h in range(2):
                v = y_buf[r, s, t, 2 * j + h].astype(F32)
                pair.append((v[0].reshape(WIN, 8, LANES), v[1].reshape(WIN, 8, LANES)))
            for a in range(8):
                reals = []
                imags = []
                for yr, yi in pair:
                    re = im = None
                    for w in range(WIN):
                        xr = xf[0, pl.ds(w * 8 + a, 1), :]
                        xi = xf[1, pl.ds(w * 8 + a, 1), :]
                        p = xr * yr[w] + xi * yi[w]
                        q = xi * yr[w] - xr * yi[w]
                        re = p if re is None else re + p
                        im = q if im is None else im + q
                    reals.append(re)
                    imags.append(im)
                rows = pl.ds(pl.multiple_of(a * BLK + 16 * j, 16), 16)
                at = 2 * LANES * n
                lhs[rows, at:at + LANES] = jnp.concatenate(reals, 0).astype(BF16)
                lhs[rows, at + LANES:at + 2 * LANES] = jnp.concatenate(imags, 0).astype(BF16)
            return carry

        lax.fori_loop(0, 4, body, 0)

    def all_tables(t, carry):
        for n in range(8):
            table_copy(t, n).start()
        return carry

    def all_out(t, carry):
        each_start(t, True)
        return carry

    lax.fori_loop(0, steps, all_out, 0)
    lax.fori_loop(0, steps, all_tables, 0)
    enter(0)
    o_ref[...] = jnp.zeros_like(o_ref)

    def step(t, carry):
        cross(t, 0)

        @pl.when(t < steps - 1)
        def _():
            enter(t + 1)

        arrived(y_buf.at[0, 1, t], y_sem.at[0, 1, t])
        cross(t, 1)
        arrived(y_buf.at[3, 0, t], y_sem.at[3, 0, t])
        arrived(y_buf.at[1, 0, t], y_sem.at[1, 0, t])
        for copy in y_second(t):
            copy.start()
        cross(t, 2)
        cross(t, 3)
        arrived(y_buf.at[1, 1, t], y_sem.at[1, 1, t])
        cross(t, 4)
        arrived(y_buf.at[2, 0, t], y_sem.at[2, 0, t])
        for copy in y_third(t):
            copy.start()
        arrived(y_buf.at[3, 1, t], y_sem.at[3, 1, t])
        cross(t, 5)
        cross(t, 6)
        arrived(y_buf.at[2, 1, t], y_sem.at[2, 1, t])
        cross(t, 7)
        for n in range(8):
            table_copy(t, n).wait()

        def columns(i, inner):
            cols = pl.ds(pl.multiple_of(i * 256, 256), 256)
            o_ref[:, cols] += jnp.dot(lhs[...], table[t, :, cols], preferred_element_type=F32) * norm
            return inner

        lax.fori_loop(0, LAGS // 256, columns, 0)
        return carry

    lax.fori_loop(0, steps, step, 0)

    def drain(t, carry):
        each_start(t, False)

        @pl.when(x_pass)
        def _():
            x_relay(t).wait_send()

        @pl.when(y_pass)
        def _():
            y_relay(t).wait_send()

        for copy in y_first(t) + y_second(t) + y_third(t):
            copy.wait_send()
        for copy in x_copies(t):
            copy.wait_send()
        return carry

    lax.fori_loop(0, steps, drain, 0)


def on_device(rows_z, parts, spectra, pair_blocks):
    del pair_blocks
    bins_local = spectra.shape[3]
    steps = bins_local // LANES
    bins_total = bins_local * parts
    norm = 1.0 / math.sqrt(WIN * bins_total)
    table = jnp.asarray(table_pieces(parts, steps, bins_total))
    pieces = spectra.reshape(WIN, 8, 8, 2, steps, LANES).transpose(4, 1, 3, 0, 2, 5)
    pieces = pieces.reshape(steps, 8, 2, BLK, LANES)
    dma = pltpu.SemaphoreType.DMA
    out = pl.pallas_call(
        functools.partial(kernel, rows_z, steps, norm),
        out_shape=jax.ShapeDtypeStruct((8 * BLK, LAGS), F32),
        in_specs=[pl.BlockSpec(memory_space=pl.ANY)] * 2,
        out_specs=pl.BlockSpec(memory_space=pltpu.VMEM),
        scratch_shapes=[
            pltpu.VMEM((4, 2, steps, 8, 2, BLK, LANES), BF16),
            pltpu.VMEM((steps, 8, 2, BLK, LANES), BF16),
            pltpu.VMEM((4, 2, steps, 2, BLK, LANES), BF16),
            pltpu.VMEM((steps, 16 * LANES, LAGS), BF16),
            pltpu.VMEM((8 * BLK, 16 * LANES), BF16),
            pltpu.VMEM((2, BLK, LANES), F32),
            dma((steps,)), dma((steps,)), dma((4, 2, steps)), dma((4, 2, steps)), dma((steps, 8)),
            dma((steps,)), dma((steps,)), dma((steps, 2)), dma((steps, 2)), dma((steps, 8)), dma((steps, 8)),
        ],
        compiler_params=pltpu.CompilerParams(
            collective_id=0, has_side_effects=True, vmem_limit_bytes=52 * 1024 * 1024),
        cost_estimate=pl.CostEstimate(flops=9_000_000_000, bytes_accessed=24_000_000, transcendentals=0),
    )(pieces, table)
    return out.reshape(8, 1, BLK, LAGS)


def solution(mesh):
    rows_z = mesh.shape["sta"] // NY
    return jax.shard_map(
        functools.partial(on_device, rows_z, mesh.shape["freq"]),
        mesh=mesh,
        in_specs=(P(None, "sta", None, "freq"), P("sta", None)),
        out_specs=P("freq", "sta", None, None),
        check_vma=False,
    )
```

```python
import functools
import math

import jax
import jax.numpy as jnp
import ml_dtypes
import numpy as np
from jax import lax
from jax.experimental import pallas as pl
from jax.experimental.pallas import tpu as pltpu
from jax.sharding import PartitionSpec as P

LAGS = 1024
WIN = 8
BLK = 64
NY = 4
LANES = 128
MESH = pl.DeviceIdType.MESH
F32 = jnp.float32
BF16 = jnp.bfloat16

OWN, MATE, FAR, FARMATE = range(4)


def table_pieces(parts, steps, bins_total):
    fft_length = 2 * bins_total
    bins = np.arange(bins_total, dtype=np.int64)
    lags = np.arange(LAGS, dtype=np.int64) - LAGS // 2
    angles = ((bins[:, None] * lags[None, :]) % fft_length) * (2.0 * math.pi / fft_length)
    both = np.stack([np.cos(angles), -np.sin(angles)]).astype(np.float32)
    both = both.reshape(2, parts, steps, LANES, LAGS).transpose(1, 2, 0, 3, 4)
    return both.reshape(parts, steps, 2 * LANES, LAGS).astype(ml_dtypes.bfloat16)


def kernel(rows_z, steps, norm, s_ref, t_ref, o_ref, y_buf, x_in, x_buf, table, lhs, xf, acc, r_out, r_in,
           xz_sem, yz_sem, y_sem, x_sem, t_sem, xo_sem, yo_sem, xe_sem, ye_sem, ys_sem, xs_sem, ro_sem, ri_sem):
    sta = lax.axis_index("sta")
    me = lax.axis_index("freq")
    z = sta // NY
    yy = sta % NY
    chip = me // 2
    core = me % 2
    last = rows_z * NY - 1
    turn = 1 - 2 * (chip % 2)
    side = ((chip + turn + 4) % 4, (chip - turn + 4) % 4)
    across = (chip + 2) % 4
    mate = me + 1 - 2 * core

    def at(where, other):
        return 2 * where + (core + other) % 2

    x_low = z == 0
    y_high = z == rows_z - 1
    x_src = sta == 0
    y_src = sta == last
    x_pass = jnp.logical_and(x_low, yy % 2 == 1)
    y_pass = jnp.logical_and(y_high, yy % 2 == 0)
    x_half = jnp.where(yy == 1, 0, 4)
    y_half = jnp.where(yy == 2, 0, 4)

    barrier = pltpu.get_barrier_semaphore()

    def greet(row, col):
        pl.semaphore_signal(barrier, inc=1, device_id=(row, col), device_id_type=MESH)

    greet(sta, mate)
    for h in range(2):
        for other in range(2):
            greet(sta, at(side[h], other))

    @pl.when(z > 0)
    def _():
        greet(sta - NY, me)

    @pl.when(z < rows_z - 1)
    def _():
        greet(sta + NY, me)

    @pl.when(x_pass)
    def _():
        greet(0, me)

    @pl.when(jnp.logical_and(x_low, yy == 2))
    def _():
        greet(1, me)
        greet(3, me)

    @pl.when(y_pass)
    def _():
        greet(last, me)

    @pl.when(jnp.logical_and(y_high, yy == 1))
    def _():
        greet(last - 1, me)
        greet(last - 3, me)

    expected = 5
    for flag, count in ((z < rows_z - 1, 1), (z > 0, 1), (x_src, 2), (y_src, 2), (x_pass, 1), (y_pass, 1)):
        expected = expected + jnp.where(flag, count, 0)
    pl.semaphore_wait(barrier, expected)

    def remote(src, dst, send, recv, row, col):
        return pltpu.make_async_remote_copy(
            src_ref=src, dst_ref=dst, send_sem=send, recv_sem=recv,
            device_id=(row, col), device_id_type=MESH)

    def x_out(t):
        return remote(s_ref.at[t], x_in.at[t], xo_sem.at[t], xz_sem.at[t], sta + NY, me)

    def y_out(t):
        return remote(s_ref.at[t], y_buf.at[OWN, t], yo_sem.at[t], yz_sem.at[t], sta - NY, me)

    def x_edge(t, n):
        return remote(s_ref.at[t], x_in.at[t], xe_sem.at[t, n], xz_sem.at[t], 1 + 2 * n, me)

    def y_edge(t, n):
        return remote(s_ref.at[t], y_buf.at[OWN, t], ye_sem.at[t, n], yz_sem.at[t], last - 1 - 2 * n, me)

    def x_own(t):
        return pltpu.make_async_copy(s_ref.at[t], x_in.at[t], xz_sem.at[t])

    def y_own(t):
        return pltpu.make_async_copy(s_ref.at[t], y_buf.at[OWN, t], yz_sem.at[t])

    def x_relay(t):
        piece = x_in.at[t, pl.ds(x_half, 4)]
        return remote(piece, piece, xe_sem.at[t, 0], xz_sem.at[t], 2, me)

    def y_relay(t):
        piece = y_buf.at[OWN, t, pl.ds(y_half, 4)]
        return remote(piece, piece, ye_sem.at[t, 0], yz_sem.at[t], last - 2, me)

    def y_sides(t):
        return [remote(y_buf.at[OWN, t, pl.ds(4 * h, 4)], y_buf.at[FAR, t, pl.ds(4 * h, 4)], ys_sem.at[t, h],
                       y_sem.at[FAR, t], sta, at(side[h], 0)) for h in range(2)]

    def y_mate(t):
        return remote(y_buf.at[OWN, t], y_buf.at[MATE, t], ys_sem.at[t, 2], y_sem.at[MATE, t], sta, mate)

    def y_far(t):
        return remote(y_buf.at[FAR, t], y_buf.at[FARMATE, t], ys_sem.at[t, 3], y_sem.at[FARMATE, t], sta, mate)

    def x_sides(t):
        copies = []
        for h in range(2):
            for g, where in enumerate((side[h], across)):
                for other in range(2):
                    source = FAR + other
                    copies.append(remote(
                        x_in.at[t, at(where, other)], x_buf.at[source, t, 2 * h + g], xs_sem.at[t, 4 * h + 2 * g + other],
                        x_sem.at[source, t], sta, at(side[h], other)))
        return copies

    def x_mate(t):
        return [remote(x_in.at[t, at((chip, side[1], chip, side[0])[q], 1)], x_buf.at[MATE, t, q], xs_sem.at[t, 8 + q],
                       x_sem.at[MATE, t], sta, mate) for q in range(4)]

    def x_mine(t):
        return [pltpu.make_async_copy(x_in.at[t, at((chip, side[1], chip, side[0])[q], 0)], x_buf.at[OWN, t, q],
                                      xs_sem.at[t, 12 + q]) for q in range(4)]

    def arrived(ref, sem):
        pltpu.make_async_copy(ref, ref, sem).wait()

    def table_copy(t, n):
        chunk = at((side[0], chip, side[1])[n // 2], n % 2)
        return pltpu.make_async_copy(t_ref.at[chunk, t], table.at[t, pl.ds(2 * LANES * n, 2 * LANES)], t_sem.at[t, n])

    def each_start(t, start):
        def go(copy):
            if start:
                copy.start()
            else:
                copy.wait_send()

        @pl.when(z < rows_z - 1)
        def _():
            go(x_out(t))

        @pl.when(z > 0)
        def _():
            go(y_out(t))

        @pl.when(x_src)
        def _():
            go(x_edge(t, 0))
            go(x_edge(t, 1))
            if start:
                x_own(t).start()

        @pl.when(y_src)
        def _():
            go(y_edge(t, 0))
            go(y_edge(t, 1))
            if start:
                y_own(t).start()

    def enter(t):
        arrived(y_buf.at[OWN, t], yz_sem.at[t])
        for copy in y_sides(t):
            copy.start()
        y_mate(t).start()

        @pl.when(y_pass)
        def _():
            y_relay(t).start()

        arrived(x_in.at[t], xz_sem.at[t])
        for copy in x_sides(t) + x_mate(t) + x_mine(t):
            copy.start()

        @pl.when(x_pass)
        def _():
            x_relay(t).start()

    def second(t):
        arrived(y_buf.at[FAR, t], y_sem.at[FAR, t])
        y_far(t).start()

    def cross(t, src, g):
        for h in range(2):
            x = x_buf[src, t, 2 * h + g].astype(F32)
            xf[h, 0] = x[0]
            xf[h, 1] = x[1]
            xf[h, 2] = x[0] + x[1]

        for h in range(2):
            def body(j, carry, h=h):
                pair = []
                for k in range(2):
                    v = y_buf[src, t, 4 * h + 2 * j + k].astype(F32)
                    yr = v[0].reshape(WIN, 8, LANES)
                    yi = v[1].reshape(WIN, 8, LANES)
                    pair.append((yr, yi, yr - yi))
                for a in range(8):
                    reals = []
                    imags = []
                    for yr, yi, yd in pair:
                        u = v = d = None
                        for w in range(WIN):
                            row = pl.ds(w * 8 + a, 1)
                            uw = xf[h, 0, row, :] * yr[w]
                            vw = xf[h, 1, row, :] * yi[w]
                            dw = xf[h, 2, row, :] * yd[w]
                            u = uw if u is None else u + uw
                            v = vw if v is None else v + vw
                            d = dw if d is None else d + dw
                        reals.append(u + v)
                        imags.append(d - (u - v))
                    rows = pl.ds(pl.multiple_of(a * 32 + 16 * j, 16), 16)
                    col = 2 * LANES * ((src + 2 - 2 * h) % 4)
                    lhs[h, rows, col:col + LANES] = jnp.concatenate(reals, 0).astype(BF16)
                    lhs[h, rows, col + LANES:col + 2 * LANES] = jnp.concatenate(imags, 0).astype(BF16)
                return carry

            lax.fori_loop(0, 2, body, 0)

    def product(t, h):
        return jnp.dot(lhs[h], table[t, 4 * LANES * h:4 * LANES * h + 8 * LANES, :], preferred_element_type=F32)

    def r_copy(h):
        return remote(r_out.at[h], r_in.at[h], ro_sem.at[h], ri_sem.at[h], sta, at(side[1 - h], 0))

    def all_out(t, carry):
        each_start(t, True)
        return carry

    def all_tables(t, carry):
        for n in range(6):
            table_copy(t, n).start()
        return carry

    lax.fori_loop(0, steps, all_out, 0)
    lax.fori_loop(0, steps, all_tables, 0)
    acc[...] = jnp.zeros_like(acc)

    def near(t):
        for copy in x_mine(t):
            copy.wait()
        cross(t, OWN, 1)
        arrived(y_buf.at[MATE, t], y_sem.at[MATE, t])
        arrived(x_buf.at[MATE, t], x_sem.at[MATE, t])
        cross(t, MATE, 1)

    def far(t):
        second(t)
        arrived(x_buf.at[FAR, t], x_sem.at[FAR, t])
        cross(t, FAR, 1)
        arrived(y_buf.at[FARMATE, t], y_sem.at[FARMATE, t])
        arrived(x_buf.at[FARMATE, t], x_sem.at[FARMATE, t])
        cross(t, FARMATE, 1)
        for n in range(6):
            table_copy(t, n).wait()

    enter(0)
    near(0)

    def step(t, carry):
        enter(t)
        far(t - 1)
        for h in range(2):
            acc[1, h] += product(t - 1, h)
        near(t)
        return carry

    lax.fori_loop(1, steps, step, 0)
    far(steps - 1)
    for h in range(2):
        r_out[h] = (acc[1, h] + product(steps - 1, h)).astype(BF16)
        r_copy(h).start()

    def mine(t, carry):
        for src in range(4):
            cross(t, src, 0)
        for h in range(2):
            acc[0, h] += product(t, h)
        return carry

    lax.fori_loop(0, steps, mine, 0)

    for h in range(2):
        r_copy(h).wait_recv()
        total = (acc[0, h] + r_in[h].astype(F32)) * norm
        o_ref[:, 32 * h:32 * h + 32, :] = total.reshape(8, 32, LAGS)

    def drain(t, carry):
        each_start(t, False)

        @pl.when(x_pass)
        def _():
            x_relay(t).wait_send()

        @pl.when(y_pass)
        def _():
            y_relay(t).wait_send()

        for copy in y_sides(t) + [y_mate(t), y_far(t)] + x_sides(t) + x_mate(t):
            copy.wait_send()
        return carry

    lax.fori_loop(0, steps, drain, 0)
    for h in range(2):
        r_copy(h).wait_send()


def on_device(rows_z, parts, spectra, pair_blocks):
    del pair_blocks
    bins_local = spectra.shape[3]
    steps = bins_local // LANES
    bins_total = bins_local * parts
    norm = 1.0 / math.sqrt(WIN * bins_total)
    table = jnp.asarray(table_pieces(parts, steps, bins_total))
    pieces = spectra.reshape(WIN, 8, 8, 2, steps, LANES).transpose(4, 1, 3, 0, 2, 5)
    pieces = pieces.reshape(steps, 8, 2, BLK, LANES)
    dma = pltpu.SemaphoreType.DMA
    out = pl.pallas_call(
        functools.partial(kernel, rows_z, steps, norm),
        out_shape=jax.ShapeDtypeStruct((8, BLK, LAGS), F32),
        in_specs=[pl.BlockSpec(memory_space=pl.ANY)] * 2,
        out_specs=pl.BlockSpec(memory_space=pltpu.VMEM),
        scratch_shapes=[
            pltpu.VMEM((4, steps, 8, 2, BLK, LANES), BF16),
            pltpu.VMEM((steps, 8, 2, BLK, LANES), BF16),
            pltpu.VMEM((4, steps, 4, 2, BLK, LANES), BF16),
            pltpu.VMEM((steps, 12 * LANES, LAGS), BF16),
            pltpu.VMEM((2, 256, 8 * LANES), BF16),
            pltpu.VMEM((2, 3, BLK, LANES), F32),
            pltpu.VMEM((2, 2, 256, LAGS), F32),
            pltpu.VMEM((2, 256, LAGS), BF16),
            pltpu.VMEM((2, 256, LAGS), BF16),
            dma((steps,)), dma((steps,)), dma((4, steps)), dma((4, steps)), dma((steps, 6)),
            dma((steps,)), dma((steps,)), dma((steps, 2)), dma((steps, 2)), dma((steps, 4)), dma((steps, 16)),
            dma((2,)), dma((2,)),
        ],
        compiler_params=pltpu.CompilerParams(
            collective_id=0, has_side_effects=True, vmem_limit_bytes=52 * 1024 * 1024),
        cost_estimate=pl.CostEstimate(flops=9_000_000_000, bytes_accessed=24_000_000, transcendentals=0),
    )(pieces, table)
    return out.reshape(8, 1, BLK, LAGS)


def solution(mesh):
    rows_z = mesh.shape["sta"] // NY
    return jax.shard_map(
        functools.partial(on_device, rows_z, mesh.shape["freq"]),
        mesh=mesh,
        in_specs=(P(None, "sta", None, "freq"), P("sta", None)),
        out_specs=P("freq", "sta", None, None),
        check_vma=False,
    )
```

```python
import functools
import math

import jax
import jax.numpy as jnp
import ml_dtypes
import numpy as np
from jax import lax
from jax.experimental import pallas as pl
from jax.experimental.pallas import tpu as pltpu
from jax.sharding import PartitionSpec as P

LAGS = 1024
WIN = 8
BLK = 64
NY = 4
LANES = 128
MESH = pl.DeviceIdType.MESH
F32 = jnp.float32
BF16 = jnp.bfloat16

OWN, MATE, FAR, FARMATE = range(4)


def table_pieces(parts, steps, bins_total):
    fft_length = 2 * bins_total
    bins = np.arange(bins_total, dtype=np.int64)
    lags = np.arange(LAGS, dtype=np.int64) - LAGS // 2
    angles = ((bins[:, None] * lags[None, :]) % fft_length) * (2.0 * math.pi / fft_length)
    both = np.stack([np.cos(angles), -np.sin(angles)]).astype(np.float32)
    both = both.reshape(2, parts, steps, LANES, LAGS).transpose(1, 2, 0, 3, 4)
    return both.reshape(parts, steps, 2 * LANES, LAGS).astype(ml_dtypes.bfloat16)


def kernel(rows_z, steps, s_ref, t_ref, o_ref, r_in, y_buf, x_in, x_far, table, lhs, xf, acc, r_out,
           xz_sem, yz_sem, y_sem, x_sem, t_sem, xo_sem, yo_sem, xe_sem, ye_sem, ys_sem, xs_sem, ro_sem, ri_sem):
    sta = lax.axis_index("sta")
    me = lax.axis_index("freq")
    z = sta // NY
    yy = sta % NY
    chip = me // 2
    core = me % 2
    last = rows_z * NY - 1
    turn = 1 - 2 * (chip % 2)
    side = ((chip + turn + 4) % 4, (chip - turn + 4) % 4)
    across = (chip + 2) % 4
    mate = me + 1 - 2 * core

    def at(where, other):
        return 2 * where + (core + other) % 2

    x_low = z == 0
    y_high = z == rows_z - 1
    x_src = sta == 0
    y_src = sta == last
    x_pass = jnp.logical_and(x_low, yy % 2 == 1)
    y_pass = jnp.logical_and(y_high, yy % 2 == 0)
    x_half = jnp.where(yy == 1, 0, 4)
    y_half = jnp.where(yy == 2, 0, 4)

    barrier = pltpu.get_barrier_semaphore()

    def greet(row, col):
        pl.semaphore_signal(barrier, inc=1, device_id=(row, col), device_id_type=MESH)

    greet(sta, mate)
    for h in range(2):
        for other in range(2):
            greet(sta, at(side[h], other))

    @pl.when(z > 0)
    def _():
        greet(sta - NY, me)

    @pl.when(z < rows_z - 1)
    def _():
        greet(sta + NY, me)

    @pl.when(x_pass)
    def _():
        greet(0, me)

    @pl.when(jnp.logical_and(x_low, yy == 2))
    def _():
        greet(1, me)
        greet(3, me)

    @pl.when(y_pass)
    def _():
        greet(last, me)

    @pl.when(jnp.logical_and(y_high, yy == 1))
    def _():
        greet(last - 1, me)
        greet(last - 3, me)

    expected = 5
    for flag, count in ((z < rows_z - 1, 1), (z > 0, 1), (x_src, 2), (y_src, 2), (x_pass, 1), (y_pass, 1)):
        expected = expected + jnp.where(flag, count, 0)
    pl.semaphore_wait(barrier, expected)

    def remote(src, dst, send, recv, row, col):
        return pltpu.make_async_remote_copy(
            src_ref=src, dst_ref=dst, send_sem=send, recv_sem=recv,
            device_id=(row, col), device_id_type=MESH)

    def x_out(t):
        return remote(s_ref.at[t], x_in.at[OWN, t], xo_sem.at[t], xz_sem.at[t], sta + NY, me)

    def y_out(t):
        return remote(s_ref.at[t], y_buf.at[OWN, t], yo_sem.at[t], yz_sem.at[t], sta - NY, me)

    def x_edge(t, n):
        return remote(s_ref.at[t], x_in.at[OWN, t], xe_sem.at[t, n], xz_sem.at[t], 1 + 2 * n, me)

    def y_edge(t, n):
        return remote(s_ref.at[t], y_buf.at[OWN, t], ye_sem.at[t, n], yz_sem.at[t], last - 1 - 2 * n, me)

    def x_own(t):
        return pltpu.make_async_copy(s_ref.at[t], x_in.at[OWN, t], xz_sem.at[t])

    def y_own(t):
        return pltpu.make_async_copy(s_ref.at[t], y_buf.at[OWN, t], yz_sem.at[t])

    def x_relay(t):
        piece = x_in.at[OWN, t, pl.ds(x_half, 4)]
        return remote(piece, piece, xe_sem.at[t, 0], xz_sem.at[t], 2, me)

    def y_relay(t):
        piece = y_buf.at[OWN, t, pl.ds(y_half, 4)]
        return remote(piece, piece, ye_sem.at[t, 0], yz_sem.at[t], last - 2, me)

    def y_sides(t):
        return [remote(y_buf.at[OWN, t, pl.ds(4 * h, 4)], y_buf.at[FAR, t, pl.ds(4 * h, 4)], ys_sem.at[t, h],
                       y_sem.at[FAR, t], sta, at(side[h], 0)) for h in range(2)]

    def y_mate(t):
        return remote(y_buf.at[OWN, t], y_buf.at[MATE, t], ys_sem.at[t, 2], y_sem.at[MATE, t], sta, mate)

    def y_far(t):
        return remote(y_buf.at[FAR, t], y_buf.at[FARMATE, t], ys_sem.at[t, 3], y_sem.at[FARMATE, t], sta, mate)

    def x_sides(t):
        return [remote(x_in.at[OWN, t, pl.ds(2 * where, 2)], x_far.at[0, t, 2 * h + g], xs_sem.at[t, 2 * h + g],
                       x_sem.at[FAR, t], sta, at(side[h], 0))
                for h in range(2) for g, where in enumerate((side[h], across))]

    def x_mate(t):
        return remote(x_in.at[OWN, t], x_in.at[MATE, t], xs_sem.at[t, 4], x_sem.at[MATE, t], sta, mate)

    def x_hand(t):
        return remote(x_far.at[0, t, :, 1 - core], x_far.at[1, t, :, 1 - core], xs_sem.at[t, 5],
                      x_sem.at[FARMATE, t], sta, mate)

    def arrived(ref, sem):
        pltpu.make_async_copy(ref, ref, sem).wait()

    def table_copy(t, n):
        chunk = at((side[0], chip, side[1])[n // 2], 1 - n if n < 2 else n % 2)
        return pltpu.make_async_copy(t_ref.at[chunk, t], table.at[t, pl.ds(2 * LANES * n, 2 * LANES)], t_sem.at[t, n])

    def each_start(t, start):
        def go(copy):
            if start:
                copy.start()
            else:
                copy.wait_send()

        @pl.when(z < rows_z - 1)
        def _():
            go(x_out(t))

        @pl.when(z > 0)
        def _():
            go(y_out(t))

        @pl.when(x_src)
        def _():
            go(x_edge(t, 0))
            go(x_edge(t, 1))
            if start:
                x_own(t).start()

        @pl.when(y_src)
        def _():
            go(y_edge(t, 0))
            go(y_edge(t, 1))
            if start:
                y_own(t).start()

    def enter(t):
        arrived(y_buf.at[OWN, t], yz_sem.at[t])
        for copy in y_sides(t):
            copy.start()
        y_mate(t).start()

        @pl.when(y_pass)
        def _():
            y_relay(t).start()

        arrived(x_in.at[OWN, t], xz_sem.at[t])
        for copy in x_sides(t):
            copy.start()
        x_mate(t).start()

        @pl.when(x_pass)
        def _():
            x_relay(t).start()

    def second(t):
        arrived(y_buf.at[FAR, t], y_sem.at[FAR, t])
        y_far(t).start()
        arrived(x_far.at[0, t], x_sem.at[FAR, t])
        x_hand(t).start()

    def cross(t, src, g, out):
        for h in range(2):
            group = at(side[1 - h] if g else chip, 0)
            x = [(x_in[src, 2 * t + c, group] if src < FAR else x_far[src - FAR, 2 * t + c, 2 * h + g, core]).astype(F32)
                 for c in range(2)]
            xf[h, 0] = x[0]
            xf[h, 1] = x[1]
            xf[h, 2] = x[0] + x[1]

        for h in range(2):
            def body(j, carry, h=h):
                pair = []
                for k in range(2):
                    yr = y_buf[src, 2 * t, 4 * h + 2 * j + k].astype(F32).reshape(WIN, 8, LANES)
                    yi = y_buf[src, 2 * t + 1, 4 * h + 2 * j + k].astype(F32).reshape(WIN, 8, LANES)
                    pair.append((yr, yi, yr - yi))
                for a in range(8):
                    reals = []
                    imags = []
                    for yr, yi, yd in pair:
                        u = v = d = None
                        for w in range(WIN):
                            row = pl.ds(w * 8 + a, 1)
                            uw = xf[h, 0, row, :] * yr[w]
                            vw = xf[h, 1, row, :] * yi[w]
                            dw = xf[h, 2, row, :] * yd[w]
                            u = uw if u is None else u + uw
                            v = vw if v is None else v + vw
                            d = dw if d is None else d + dw
                        reals.append(u + v)
                        imags.append(d - (u - v))
                    rows = pl.ds(pl.multiple_of(a * 32 + 16 * j, 16), 16)
                    col = 2 * LANES * (src if h else (2, 3, 1, 0)[src])
                    out[h, rows, col:col + LANES] = jnp.concatenate(reals, 0).astype(BF16)
                    out[h, rows, col + LANES:col + 2 * LANES] = jnp.concatenate(imags, 0).astype(BF16)
                return carry

            lax.fori_loop(0, 2, body, 0)

    def product(t, h, left, first=0, count=4):
        cols = slice(2 * LANES * first, 2 * LANES * (first + count))
        bins = slice(2 * LANES * (2 * h + first), 2 * LANES * (2 * h + first + count))
        return jnp.dot(left[h, :, cols], table[t, bins, :], preferred_element_type=F32)

    def r_copy(h):
        return remote(r_out.at[h], r_in.at[:, h], ro_sem.at[h], ri_sem.at[h], sta, at(side[1 - h], 0))

    def all_out(u, carry):
        each_start(u, True)
        return carry

    def all_tables(t, carry):
        for n in range(6):
            table_copy(t, n).start()
        return carry

    lax.fori_loop(0, 2 * steps, all_out, 0)
    lax.fori_loop(0, steps, all_tables, 0)
    acc[...] = jnp.zeros_like(acc)
    o_ref[...] = jnp.zeros_like(o_ref)

    def near(t):
        cross(t, OWN, 1, lhs)
        for u in (2 * t, 2 * t + 1):
            arrived(y_buf.at[MATE, u], y_sem.at[MATE, u])
            arrived(x_in.at[MATE, u], x_sem.at[MATE, u])
        cross(t, MATE, 1, lhs)

    def far_mate(t):
        for u in (2 * t, 2 * t + 1):
            arrived(y_buf.at[FARMATE, u], y_sem.at[FARMATE, u])
            arrived(x_far.at[1, u, :, core], x_sem.at[FARMATE, u])
        cross(t, FARMATE, 1, lhs)

    def tables_here(t):
        for n in range(6):
            table_copy(t, n).wait()

    enter(0)
    enter(1)
    second(0)
    near(0)

    def step(t, carry):
        enter(2 * t)
        second(2 * t - 1)
        cross(t - 1, FAR, 1, lhs)
        enter(2 * t + 1)
        far_mate(t - 1)
        tables_here(t - 1)
        for h in range(2):
            acc[h] += product(t - 1, h, lhs)
        second(2 * t)
        near(t)
        return carry

    lax.fori_loop(1, steps, step, 0)

    end = steps - 1
    tables_here(end)
    second(2 * steps - 1)
    cross(end, FAR, 1, lhs)
    for h in range(2):
        acc[h] += product(end, h, lhs, 1 - h, 3)
    far_mate(end)
    for h in range(2):
        r_out[h] = (acc[h] + product(end, h, lhs, 3 * h, 1)).astype(BF16).reshape(8, 32, LAGS)
        r_copy(h).start()

    def mine(t, carry):
        for src in range(4):
            cross(t, src, 0, lhs)
        for h in range(2):
            o_ref[:, h] += product(t, h, lhs).reshape(8, 32, LAGS)
        return carry

    lax.fori_loop(0, steps, mine, 0)

    def drain(u, carry):
        each_start(u, False)

        @pl.when(x_pass)
        def _():
            x_relay(u).wait_send()

        @pl.when(y_pass)
        def _():
            y_relay(u).wait_send()

        for copy in y_sides(u) + [y_mate(u), y_far(u)] + x_sides(u) + [x_mate(u), x_hand(u)]:
            copy.wait_send()
        return carry

    lax.fori_loop(0, 2 * steps, drain, 0)
    for h in range(2):
        r_copy(h).wait()


def finish(norm, own_ref, others_ref, o_ref, buf, sem):
    def out(a):
        return pltpu.make_async_copy(buf.at[a], o_ref.at[a], sem.at[a])

    for a in range(8):
        buf[a] = (own_ref[a] + others_ref[a].astype(F32)) * norm
        out(a).start()
    for a in range(8):
        out(a).wait()


def on_device(rows_z, parts, spectra, pair_blocks):
    del pair_blocks
    bins_local = spectra.shape[3]
    steps = bins_local // LANES
    bins_total = bins_local * parts
    norm = 1.0 / math.sqrt(WIN * bins_total)
    table = jnp.asarray(table_pieces(parts, steps, bins_total))
    pieces = spectra.reshape(WIN, 8, 8, 2, steps, LANES).transpose(4, 3, 1, 0, 2, 5)
    pieces = pieces.reshape(2 * steps, 8, BLK, LANES)
    dma = pltpu.SemaphoreType.DMA
    own, others = pl.pallas_call(
        functools.partial(kernel, rows_z, steps),
        out_shape=(jax.ShapeDtypeStruct((8, 2, 32, LAGS), F32), jax.ShapeDtypeStruct((8, 2, 32, LAGS), BF16)),
        in_specs=[pl.BlockSpec(memory_space=pl.ANY)] * 2,
        out_specs=(pl.BlockSpec(memory_space=pltpu.VMEM),) * 2,
        scratch_shapes=[
            pltpu.VMEM((4, 2 * steps, 8, BLK, LANES), BF16),
            pltpu.VMEM((2, 2 * steps, 8, BLK, LANES), BF16),
            pltpu.VMEM((2, 2 * steps, 4, 2, BLK, LANES), BF16),
            pltpu.VMEM((steps, 12 * LANES, LAGS), BF16),
            pltpu.VMEM((2, 256, 8 * LANES), BF16),
            pltpu.VMEM((2, 3, BLK, LANES), F32),
            pltpu.VMEM((2, 256, LAGS), F32),
            pltpu.VMEM((2, 8, 32, LAGS), BF16),
            dma((2 * steps,)), dma((2 * steps,)), dma((4, 2 * steps)), dma((4, 2 * steps)), dma((steps, 6)),
            dma((2 * steps,)), dma((2 * steps,)), dma((2 * steps, 2)), dma((2 * steps, 2)),
            dma((2 * steps, 4)), dma((2 * steps, 6)), dma((2,)), dma((2,)),
        ],
        compiler_params=pltpu.CompilerParams(
            collective_id=0, has_side_effects=True, vmem_limit_bytes=44 * 1024 * 1024),
        cost_estimate=pl.CostEstimate(flops=9_000_000_000, bytes_accessed=24_000_000, transcendentals=0),
    )(pieces, table)
    out = pl.pallas_call(
        functools.partial(finish, norm),
        out_shape=jax.ShapeDtypeStruct((8, 2, 32, LAGS), F32),
        in_specs=[pl.BlockSpec(memory_space=pltpu.VMEM)] * 2,
        out_specs=pl.BlockSpec(memory_space=pl.ANY),
        scratch_shapes=[pltpu.VMEM((8, 2, 32, LAGS), F32), dma((8,))],
        compiler_params=pltpu.CompilerParams(vmem_limit_bytes=8 * 1024 * 1024),
    )(own, others)
    return out.reshape(8, 1, BLK, LAGS)


def solution(mesh):
    rows_z = mesh.shape["sta"] // NY
    return jax.shard_map(
        functools.partial(on_device, rows_z, mesh.shape["freq"]),
        mesh=mesh,
        in_specs=(P(None, "sta", None, "freq"), P("sta", None)),
        out_specs=P("freq", "sta", None, None),
        check_vma=False,
    )
```

```python
import functools
import math

import jax
import jax.numpy as jnp
import ml_dtypes
import numpy as np
from jax import lax
from jax.experimental import pallas as pl
from jax.experimental.pallas import tpu as pltpu
from jax.sharding import PartitionSpec as P

LAGS = 1024
WIN = 8
BLK = 64
NY = 4
LANES = 128
MESH = pl.DeviceIdType.MESH
F32 = jnp.float32
BF16 = jnp.bfloat16

OWN, MATE, FAR, FARMATE = range(4)


def table_pieces(parts, steps, bins_total):
    fft_length = 2 * bins_total
    bins = np.arange(bins_total, dtype=np.int64)
    lags = np.arange(LAGS, dtype=np.int64) - LAGS // 2
    angles = ((bins[:, None] * lags[None, :]) % fft_length) * (2.0 * math.pi / fft_length)
    both = np.stack([np.cos(angles), -np.sin(angles)]).astype(np.float32)
    both = both.reshape(2, parts, steps, LANES, LAGS).transpose(1, 2, 0, 3, 4)
    return both.reshape(parts, steps, 2 * LANES, LAGS).astype(ml_dtypes.bfloat16)


def kernel(rows_z, steps, s_ref, t_ref, o_ref, r_in, y_buf, x_in, x_far, table, lhs, xf, acc, r_out,
           xz_sem, yz_sem, xr_sem, yr_sem, y_sem, x_sem, t_sem, xo_sem, yo_sem, xe_sem, ye_sem, ys_sem, xs_sem, ro_sem, ri_sem):
    sta = lax.axis_index("sta")
    me = lax.axis_index("freq")
    z = sta // NY
    yy = sta % NY
    chip = me // 2
    core = me % 2
    last = rows_z * NY - 1
    turn = 1 - 2 * (chip % 2)
    side = ((chip + turn + 4) % 4, (chip - turn + 4) % 4)
    across = (chip + 2) % 4
    mate = me + 1 - 2 * core

    def at(where, other):
        return 2 * where + (core + other) % 2

    x_low = z == 0
    y_high = z == rows_z - 1
    x_src = sta == 0
    y_src = sta == last
    x_pass = jnp.logical_and(x_low, yy % 2 == 1)
    y_pass = jnp.logical_and(y_high, yy % 2 == 0)
    x_half = jnp.where(yy == 1, 0, 4)
    y_half = jnp.where(yy == 2, 0, 4)

    barrier = pltpu.get_barrier_semaphore()

    def greet(row, col):
        pl.semaphore_signal(barrier, inc=1, device_id=(row, col), device_id_type=MESH)

    greet(sta, mate)
    for h in range(2):
        for other in range(2):
            greet(sta, at(side[h], other))

    @pl.when(z > 0)
    def _():
        greet(sta - NY, me)

    @pl.when(z < rows_z - 1)
    def _():
        greet(sta + NY, me)

    @pl.when(x_pass)
    def _():
        greet(0, me)

    @pl.when(jnp.logical_and(x_low, yy == 2))
    def _():
        greet(1, me)
        greet(3, me)

    @pl.when(y_pass)
    def _():
        greet(last, me)

    @pl.when(jnp.logical_and(y_high, yy == 1))
    def _():
        greet(last - 1, me)
        greet(last - 3, me)

    expected = 5
    for flag, count in ((z < rows_z - 1, 1), (z > 0, 1), (x_src, 2), (y_src, 2), (x_pass, 1), (y_pass, 1)):
        expected = expected + jnp.where(flag, count, 0)
    pl.semaphore_wait(barrier, expected)

    def remote(src, dst, send, recv, row, col):
        return pltpu.make_async_remote_copy(
            src_ref=src, dst_ref=dst, send_sem=send, recv_sem=recv,
            device_id=(row, col), device_id_type=MESH)

    def x_out(t):
        return remote(s_ref.at[t], x_in.at[OWN, t], xo_sem.at[t], xz_sem.at[t], sta + NY, me)

    def y_out(t):
        return remote(s_ref.at[t], y_buf.at[OWN, t], yo_sem.at[t], yz_sem.at[t], sta - NY, me)

    def x_edge(t, n):
        return [remote(s_ref.at[t, pl.ds(lo, 4)], x_in.at[OWN, t, pl.ds(lo, 4)], xe_sem.at[t, 2 * n + i],
                       (xr_sem, xz_sem)[i].at[t], 1 + 2 * n, me) for i, lo in enumerate((4 * n, 4 - 4 * n))]

    def y_edge(t, n):
        return [remote(s_ref.at[t, pl.ds(lo, 4)], y_buf.at[OWN, t, pl.ds(lo, 4)], ye_sem.at[t, 2 * n + i],
                       (yr_sem, yz_sem)[i].at[t], last - 1 - 2 * n, me) for i, lo in enumerate((4 * n, 4 - 4 * n))]

    def x_own(t):
        return pltpu.make_async_copy(s_ref.at[t], x_in.at[OWN, t], xz_sem.at[t])

    def y_own(t):
        return pltpu.make_async_copy(s_ref.at[t], y_buf.at[OWN, t], yz_sem.at[t])

    def x_relay(t):
        piece = x_in.at[OWN, t, pl.ds(x_half, 4)]
        return remote(piece, piece, xe_sem.at[t, 0], xz_sem.at[t], 2, me)

    def y_relay(t):
        piece = y_buf.at[OWN, t, pl.ds(y_half, 4)]
        return remote(piece, piece, ye_sem.at[t, 0], yz_sem.at[t], last - 2, me)

    def y_sides(t):
        return [remote(y_buf.at[OWN, t, pl.ds(4 * h, 4)], y_buf.at[FAR, t, pl.ds(4 * h, 4)], ys_sem.at[t, h],
                       y_sem.at[FAR, t], sta, at(side[h], 0)) for h in range(2)]

    def y_mate(t):
        return remote(y_buf.at[OWN, t], y_buf.at[MATE, t], ys_sem.at[t, 2], y_sem.at[MATE, t], sta, mate)

    def y_far(t):
        return remote(y_buf.at[FAR, t], y_buf.at[FARMATE, t], ys_sem.at[t, 3], y_sem.at[FARMATE, t], sta, mate)

    def x_sides(t):
        return [remote(x_in.at[OWN, t, pl.ds(2 * where, 2)], x_far.at[0, t, 2 * h + g], xs_sem.at[t, 2 * h + g],
                       x_sem.at[FAR, t], sta, at(side[h], 0))
                for h in range(2) for g, where in enumerate((side[h], across))]

    def x_mate(t):
        return remote(x_in.at[OWN, t], x_in.at[MATE, t], xs_sem.at[t, 4], x_sem.at[MATE, t], sta, mate)

    def x_hand(t):
        return remote(x_far.at[0, t, :, 1 - core], x_far.at[1, t, :, 1 - core], xs_sem.at[t, 5],
                      x_sem.at[FARMATE, t], sta, mate)

    def arrived(ref, sem):
        pltpu.make_async_copy(ref, ref, sem).wait()

    def table_copy(t, n):
        chunk = at((side[0], chip, side[1])[n // 2], 1 - n if n < 2 else n % 2)
        return pltpu.make_async_copy(t_ref.at[chunk, t], table.at[t, pl.ds(2 * LANES * n, 2 * LANES)], t_sem.at[t, n])

    def each_start(t, start):
        def go(copy):
            if start:
                copy.start()
            else:
                copy.wait_send()

        @pl.when(z < rows_z - 1)
        def _():
            go(x_out(t))

        @pl.when(z > 0)
        def _():
            go(y_out(t))

        @pl.when(x_src)
        def _():
            for copy in x_edge(t, 0) + x_edge(t, 1):
                go(copy)
            if start:
                x_own(t).start()

        @pl.when(y_src)
        def _():
            for copy in y_edge(t, 0) + y_edge(t, 1):
                go(copy)
            if start:
                y_own(t).start()

    def early(t):
        @pl.when(y_pass)
        def _():
            arrived(y_buf.at[OWN, t, pl.ds(0, 4)], yr_sem.at[t])
            y_relay(t).start()

        @pl.when(x_pass)
        def _():
            arrived(x_in.at[OWN, t, pl.ds(0, 4)], xr_sem.at[t])
            x_relay(t).start()

    def enter(t):
        @pl.when(y_pass)
        def _():
            arrived(y_buf.at[OWN, t, pl.ds(0, 4)], yz_sem.at[t])

        @pl.when(jnp.logical_not(y_pass))
        def _():
            arrived(y_buf.at[OWN, t], yz_sem.at[t])

        for copy in y_sides(t):
            copy.start()
        y_mate(t).start()

        @pl.when(x_pass)
        def _():
            arrived(x_in.at[OWN, t, pl.ds(0, 4)], xz_sem.at[t])

        @pl.when(jnp.logical_not(x_pass))
        def _():
            arrived(x_in.at[OWN, t], xz_sem.at[t])

        for copy in x_sides(t):
            copy.start()
        x_mate(t).start()

    def second(t):
        arrived(y_buf.at[FAR, t], y_sem.at[FAR, t])
        y_far(t).start()
        arrived(x_far.at[0, t], x_sem.at[FAR, t])
        x_hand(t).start()

    def cross(t, src, g, out):
        for h in range(2):
            group = at(side[1 - h] if g else chip, 0)
            x = [(x_in[src, 2 * t + c, group] if src < FAR else x_far[src - FAR, 2 * t + c, 2 * h + g, core]).astype(F32)
                 for c in range(2)]
            xf[h, 0] = x[0]
            xf[h, 1] = x[1]
            xf[h, 2] = x[0] + x[1]

        for h in range(2):
            def body(j, carry, h=h):
                pair = []
                for k in range(2):
                    yr = y_buf[src, 2 * t, 4 * h + 2 * j + k].astype(F32).reshape(WIN, 8, LANES)
                    yi = y_buf[src, 2 * t + 1, 4 * h + 2 * j + k].astype(F32).reshape(WIN, 8, LANES)
                    pair.append((yr, yi, yr - yi))
                for a in range(8):
                    reals = []
                    imags = []
                    for yr, yi, yd in pair:
                        u = v = d = None
                        for w in range(WIN):
                            row = pl.ds(w * 8 + a, 1)
                            uw = xf[h, 0, row, :] * yr[w]
                            vw = xf[h, 1, row, :] * yi[w]
                            dw = xf[h, 2, row, :] * yd[w]
                            u = uw if u is None else u + uw
                            v = vw if v is None else v + vw
                            d = dw if d is None else d + dw
                        reals.append(u + v)
                        imags.append(d - (u - v))
                    rows = pl.ds(pl.multiple_of(a * 32 + 16 * j, 16), 16)
                    col = 2 * LANES * (src if h else (2, 3, 1, 0)[src])
                    out[h, rows, col:col + LANES] = jnp.concatenate(reals, 0).astype(BF16)
                    out[h, rows, col + LANES:col + 2 * LANES] = jnp.concatenate(imags, 0).astype(BF16)
                return carry

            lax.fori_loop(0, 2, body, 0)

    def product(t, h, left, first=0, count=4):
        cols = slice(2 * LANES * first, 2 * LANES * (first + count))
        bins = slice(2 * LANES * (2 * h + first), 2 * LANES * (2 * h + first + count))
        return jnp.dot(left[h, :, cols], table[t, bins, :], preferred_element_type=F32)

    def r_copy(h):
        return remote(r_out.at[h], r_in.at[:, h], ro_sem.at[h], ri_sem.at[h], sta, at(side[1 - h], 0))

    def all_out(u, carry):
        each_start(u, True)
        return carry

    def all_tables(t, carry):
        for n in range(6):
            table_copy(t, n).start()
        return carry

    lax.fori_loop(0, 2 * steps, all_out, 0)
    lax.fori_loop(0, steps, all_tables, 0)
    acc[...] = jnp.zeros_like(acc)
    o_ref[...] = jnp.zeros_like(o_ref)

    def near(t):
        cross(t, OWN, 1, lhs)
        for u in (2 * t, 2 * t + 1):
            arrived(y_buf.at[MATE, u], y_sem.at[MATE, u])
            arrived(x_in.at[MATE, u], x_sem.at[MATE, u])
        cross(t, MATE, 1, lhs)

    def far_mate(t):
        for u in (2 * t, 2 * t + 1):
            arrived(y_buf.at[FARMATE, u], y_sem.at[FARMATE, u])
            arrived(x_far.at[1, u, :, core], x_sem.at[FARMATE, u])
        cross(t, FARMATE, 1, lhs)

    def tables_here(t):
        for n in range(6):
            table_copy(t, n).wait()

    early(0)
    enter(0)
    early(1)
    enter(1)
    second(0)
    early(2)
    near(0)

    def step(t, carry):
        enter(2 * t)
        second(2 * t - 1)
        early(2 * t + 1)
        cross(t - 1, FAR, 1, lhs)
        enter(2 * t + 1)
        far_mate(t - 1)
        tables_here(t - 1)
        for h in range(2):
            acc[h] += product(t - 1, h, lhs)
        second(2 * t)

        @pl.when(t < steps - 1)
        def _():
            early(2 * t + 2)

        near(t)
        return carry

    lax.fori_loop(1, steps, step, 0)

    end = steps - 1
    tables_here(end)
    second(2 * steps - 1)
    cross(end, FAR, 1, lhs)
    for h in range(2):
        acc[h] += product(end, h, lhs, 1 - h, 3)
    far_mate(end)
    for h in range(2):
        r_out[h] = (acc[h] + product(end, h, lhs, 3 * h, 1)).astype(BF16).reshape(8, 32, LAGS)
        r_copy(h).start()

    def mine(t, carry):
        for src in range(4):
            cross(t, src, 0, lhs)
        for h in range(2):
            o_ref[:, h] += product(t, h, lhs).reshape(8, 32, LAGS)
        return carry

    lax.fori_loop(0, steps, mine, 0)

    def drain(u, carry):
        each_start(u, False)

        @pl.when(x_pass)
        def _():
            x_relay(u).wait_send()

        @pl.when(y_pass)
        def _():
            y_relay(u).wait_send()

        for copy in y_sides(u) + [y_mate(u), y_far(u)] + x_sides(u) + [x_mate(u), x_hand(u)]:
            copy.wait_send()
        return carry

    lax.fori_loop(0, 2 * steps, drain, 0)
    for h in range(2):
        r_copy(h).wait()


def finish(norm, own_ref, others_ref, o_ref, buf, sem):
    def out(a):
        return pltpu.make_async_copy(buf.at[a], o_ref.at[a], sem.at[a])

    for a in range(8):
        buf[a] = (own_ref[a] + others_ref[a].astype(F32)) * norm
        out(a).start()
    for a in range(8):
        out(a).wait()


def on_device(rows_z, parts, spectra, pair_blocks):
    del pair_blocks
    bins_local = spectra.shape[3]
    steps = bins_local // LANES
    bins_total = bins_local * parts
    norm = 1.0 / math.sqrt(WIN * bins_total)
    table = jnp.asarray(table_pieces(parts, steps, bins_total))
    pieces = spectra.reshape(WIN, 8, 8, 2, steps, LANES).transpose(4, 3, 1, 0, 2, 5)
    pieces = pieces.reshape(2 * steps, 8, BLK, LANES)
    dma = pltpu.SemaphoreType.DMA
    own, others = pl.pallas_call(
        functools.partial(kernel, rows_z, steps),
        out_shape=(jax.ShapeDtypeStruct((8, 2, 32, LAGS), F32), jax.ShapeDtypeStruct((8, 2, 32, LAGS), BF16)),
        in_specs=[pl.BlockSpec(memory_space=pl.ANY)] * 2,
        out_specs=(pl.BlockSpec(memory_space=pltpu.VMEM),) * 2,
        scratch_shapes=[
            pltpu.VMEM((4, 2 * steps, 8, BLK, LANES), BF16),
            pltpu.VMEM((2, 2 * steps, 8, BLK, LANES), BF16),
            pltpu.VMEM((2, 2 * steps, 4, 2, BLK, LANES), BF16),
            pltpu.VMEM((steps, 12 * LANES, LAGS), BF16),
            pltpu.VMEM((2, 256, 8 * LANES), BF16),
            pltpu.VMEM((2, 3, BLK, LANES), F32),
            pltpu.VMEM((2, 256, LAGS), F32),
            pltpu.VMEM((2, 8, 32, LAGS), BF16),
            dma((2 * steps,)), dma((2 * steps,)), dma((2 * steps,)), dma((2 * steps,)),
            dma((4, 2 * steps)), dma((4, 2 * steps)), dma((steps, 6)),
            dma((2 * steps,)), dma((2 * steps,)), dma((2 * steps, 4)), dma((2 * steps, 4)),
            dma((2 * steps, 4)), dma((2 * steps, 6)), dma((2,)), dma((2,)),
        ],
        compiler_params=pltpu.CompilerParams(
            collective_id=0, has_side_effects=True, vmem_limit_bytes=44 * 1024 * 1024),
        cost_estimate=pl.CostEstimate(flops=9_000_000_000, bytes_accessed=24_000_000, transcendentals=0),
    )(pieces, table)
    out = pl.pallas_call(
        functools.partial(finish, norm),
        out_shape=jax.ShapeDtypeStruct((8, 2, 32, LAGS), F32),
        in_specs=[pl.BlockSpec(memory_space=pltpu.VMEM)] * 2,
        out_specs=pl.BlockSpec(memory_space=pl.ANY),
        scratch_shapes=[pltpu.VMEM((8, 2, 32, LAGS), F32), dma((8,))],
        compiler_params=pltpu.CompilerParams(vmem_limit_bytes=8 * 1024 * 1024),
    )(own, others)
    return out.reshape(8, 1, BLK, LAGS)


def solution(mesh):
    rows_z = mesh.shape["sta"] // NY
    return jax.shard_map(
        functools.partial(on_device, rows_z, mesh.shape["freq"]),
        mesh=mesh,
        in_specs=(P(None, "sta", None, "freq"), P("sta", None)),
        out_specs=P("freq", "sta", None, None),
        check_vma=False,
    )
```

```python
import functools
import math

import jax
import jax.numpy as jnp
import ml_dtypes
import numpy as np
from jax import lax
from jax.experimental import pallas as pl
from jax.experimental.pallas import tpu as pltpu
from jax.sharding import PartitionSpec as P

LAGS = 1024
WIN = 8
BLK = 64
NY = 4
LANES = 128
MESH = pl.DeviceIdType.MESH
F32 = jnp.float32
BF16 = jnp.bfloat16

OWN, MATE, FAR, FARMATE = range(4)


def table_pieces(parts, steps, bins_total):
    fft_length = 2 * bins_total
    bins = np.arange(bins_total, dtype=np.int64)
    lags = np.arange(LAGS, dtype=np.int64) - LAGS // 2
    angles = ((bins[:, None] * lags[None, :]) % fft_length) * (2.0 * math.pi / fft_length)
    both = np.stack([np.cos(angles), -np.sin(angles)]).astype(np.float32)
    both = both.reshape(2, parts, steps, LANES, LAGS).transpose(1, 2, 0, 3, 4)
    return both.reshape(parts, steps, 2 * LANES, LAGS).astype(ml_dtypes.bfloat16)


def kernel(rows_z, steps, s_ref, t_ref, o_ref, r_in, y_buf, x_in, x_far, table, lhs, xf, acc, r_out,
           xz_sem, yz_sem, xr_sem, yr_sem, y_sem, x_sem, t_sem, xo_sem, yo_sem, xe_sem, ye_sem, ys_sem, xs_sem, ro_sem, ri_sem):
    sta = lax.axis_index("sta")
    me = lax.axis_index("freq")
    z = sta // NY
    yy = sta % NY
    chip = me // 2
    core = me % 2
    last = rows_z * NY - 1
    turn = 1 - 2 * (chip % 2)
    side = ((chip + turn + 4) % 4, (chip - turn + 4) % 4)
    across = (chip + 2) % 4
    mate = me + 1 - 2 * core

    def at(where, other):
        return 2 * where + (core + other) % 2

    beside = [at(side[h], 0) for h in range(2)]
    x_low = z == 0
    y_high = z == rows_z - 1
    x_src = sta == 0
    y_src = sta == last
    x_pass = jnp.logical_and(x_low, yy % 2 == 1)
    y_pass = jnp.logical_and(y_high, yy % 2 == 0)
    x_half = jnp.where(yy == 1, 0, 4)
    y_half = jnp.where(yy == 2, 0, 4)

    barrier = pltpu.get_barrier_semaphore()

    def greet(row, col):
        pl.semaphore_signal(barrier, inc=1, device_id=(row, col), device_id_type=MESH)

    greet(sta, mate)
    for h in range(2):
        for other in range(2):
            greet(sta, at(side[h], other))

    @pl.when(z > 0)
    def _():
        greet(sta - NY, me)

    @pl.when(z < rows_z - 1)
    def _():
        greet(sta + NY, me)

    @pl.when(x_pass)
    def _():
        greet(0, me)

    @pl.when(jnp.logical_and(x_low, yy == 2))
    def _():
        greet(1, me)
        greet(3, me)

    @pl.when(y_pass)
    def _():
        greet(last, me)

    @pl.when(jnp.logical_and(y_high, yy == 1))
    def _():
        greet(last - 1, me)
        greet(last - 3, me)

    expected = 5
    for flag, count in ((z < rows_z - 1, 1), (z > 0, 1), (x_src, 2), (y_src, 2), (x_pass, 1), (y_pass, 1)):
        expected = expected + jnp.where(flag, count, 0)
    pl.semaphore_wait(barrier, expected)

    def remote(src, dst, send, recv, row, col):
        return pltpu.make_async_remote_copy(
            src_ref=src, dst_ref=dst, send_sem=send, recv_sem=recv,
            device_id=(row, col), device_id_type=MESH)

    def x_out(t):
        return remote(s_ref.at[t], x_in.at[OWN, t], xo_sem.at[t], xz_sem.at[t], sta + NY, me)

    def y_out(t):
        return remote(s_ref.at[t], y_buf.at[OWN, t], yo_sem.at[t], yz_sem.at[t], sta - NY, me)

    def x_edge(t, n):
        return [remote(s_ref.at[t, pl.ds(lo, 4)], x_in.at[OWN, t, pl.ds(lo, 4)], xe_sem.at[t, 2 * n + i],
                       (xr_sem, xz_sem)[i].at[t], 1 + 2 * n, me) for i, lo in enumerate((4 * n, 4 - 4 * n))]

    def y_edge(t, n):
        return [remote(s_ref.at[t, pl.ds(lo, 4)], y_buf.at[OWN, t, pl.ds(lo, 4)], ye_sem.at[t, 2 * n + i],
                       (yr_sem, yz_sem)[i].at[t], last - 1 - 2 * n, me) for i, lo in enumerate((4 * n, 4 - 4 * n))]

    def x_own(t):
        return pltpu.make_async_copy(s_ref.at[t], x_in.at[OWN, t], xz_sem.at[t])

    def y_own(t):
        return pltpu.make_async_copy(s_ref.at[t], y_buf.at[OWN, t], yz_sem.at[t])

    def x_relay(t):
        piece = x_in.at[OWN, t, pl.ds(x_half, 4)]
        return remote(piece, piece, xe_sem.at[t, 0], xz_sem.at[t], 2, me)

    def y_relay(t):
        piece = y_buf.at[OWN, t, pl.ds(y_half, 4)]
        return remote(piece, piece, ye_sem.at[t, 0], yz_sem.at[t], last - 2, me)

    def y_sides(t):
        return [remote(y_buf.at[OWN, t, pl.ds(4 * h, 4)], y_buf.at[FAR, t, pl.ds(4 * h, 4)], ys_sem.at[t, h],
                       y_sem.at[FAR, t], sta, beside[h]) for h in range(2)]

    def y_mate(t):
        return remote(y_buf.at[OWN, t], y_buf.at[MATE, t], ys_sem.at[t, 2], y_sem.at[MATE, t], sta, mate)

    def y_far(t):
        return remote(y_buf.at[FAR, t], y_buf.at[FARMATE, t], ys_sem.at[t, 3], y_sem.at[FARMATE, t], sta, mate)

    def x_sides(t):
        return [remote(x_in.at[OWN, t, pl.ds(2 * where, 2)], x_far.at[0, t, 2 * h + g], xs_sem.at[t, 2 * h + g],
                       x_sem.at[FAR, t], sta, beside[h])
                for h in range(2) for g, where in enumerate((side[h], across))]

    def x_mate(t):
        return remote(x_in.at[OWN, t], x_in.at[MATE, t], xs_sem.at[t, 4], x_sem.at[MATE, t], sta, mate)

    def x_hand(t):
        return remote(x_far.at[0, t, :, 1 - core], x_far.at[1, t, :, 1 - core], xs_sem.at[t, 5],
                      x_sem.at[FARMATE, t], sta, mate)

    def arrived(ref, sem):
        pltpu.make_async_copy(ref, ref, sem).wait()

    def table_copy(t, n):
        chunk = at((side[0], chip, side[1])[n // 2], 1 - n if n < 2 else n % 2)
        return pltpu.make_async_copy(t_ref.at[chunk, t], table.at[t, pl.ds(2 * LANES * n, 2 * LANES)], t_sem.at[t, n])

    def each_start(t, start):
        def go(copy):
            if start:
                copy.start()
            else:
                copy.wait_send()

        @pl.when(z < rows_z - 1)
        def _():
            go(x_out(t))

        @pl.when(z > 0)
        def _():
            go(y_out(t))

        @pl.when(x_src)
        def _():
            for copy in x_edge(t, 0) + x_edge(t, 1):
                go(copy)
            if start:
                x_own(t).start()

        @pl.when(y_src)
        def _():
            for copy in y_edge(t, 0) + y_edge(t, 1):
                go(copy)
            if start:
                y_own(t).start()

    def early(t):
        @pl.when(y_pass)
        def _():
            arrived(y_buf.at[OWN, t, pl.ds(0, 4)], yr_sem.at[t])
            y_relay(t).start()

        @pl.when(x_pass)
        def _():
            arrived(x_in.at[OWN, t, pl.ds(0, 4)], xr_sem.at[t])
            x_relay(t).start()

    def enter(t):
        @pl.when(y_pass)
        def _():
            arrived(y_buf.at[OWN, t, pl.ds(0, 4)], yz_sem.at[t])

        @pl.when(jnp.logical_not(y_pass))
        def _():
            arrived(y_buf.at[OWN, t], yz_sem.at[t])

        for copy in y_sides(t):
            copy.start()

        @pl.when(x_pass)
        def _():
            arrived(x_in.at[OWN, t, pl.ds(0, 4)], xz_sem.at[t])

        @pl.when(jnp.logical_not(x_pass))
        def _():
            arrived(x_in.at[OWN, t], xz_sem.at[t])

        for copy in x_sides(t):
            copy.start()
        y_mate(t).start()
        x_mate(t).start()

    def second(t):
        arrived(y_buf.at[FAR, t], y_sem.at[FAR, t])
        y_far(t).start()
        arrived(x_far.at[0, t], x_sem.at[FAR, t])
        x_hand(t).start()

    def cross(t, src, g, out):
        for h in range(2):
            group = at(side[1 - h] if g else chip, 0)
            x = [(x_in[src, 2 * t + c, group] if src < FAR else x_far[src - FAR, 2 * t + c, 2 * h + g, core]).astype(F32)
                 for c in range(2)]
            xf[h, 0] = x[0]
            xf[h, 1] = x[1]
            xf[h, 2] = x[0] + x[1]

        for h in range(2):
            def body(j, carry, h=h):
                pair = []
                for k in range(2):
                    yr = y_buf[src, 2 * t, 4 * h + 2 * j + k].astype(F32).reshape(WIN, 8, LANES)
                    yi = y_buf[src, 2 * t + 1, 4 * h + 2 * j + k].astype(F32).reshape(WIN, 8, LANES)
                    pair.append((yr, yi, yr - yi))
                for a in range(8):
                    reals = []
                    imags = []
                    for yr, yi, yd in pair:
                        u = v = d = None
                        for w in range(WIN):
                            row = pl.ds(w * 8 + a, 1)
                            uw = xf[h, 0, row, :] * yr[w]
                            vw = xf[h, 1, row, :] * yi[w]
                            dw = xf[h, 2, row, :] * yd[w]
                            u = uw if u is None else u + uw
                            v = vw if v is None else v + vw
                            d = dw if d is None else d + dw
                        reals.append(u + v)
                        imags.append(d - (u - v))
                    rows = pl.ds(pl.multiple_of(a * 32 + 16 * j, 16), 16)
                    col = 2 * LANES * (src if h else (2, 3, 1, 0)[src])
                    out[h, rows, col:col + LANES] = jnp.concatenate(reals, 0).astype(BF16)
                    out[h, rows, col + LANES:col + 2 * LANES] = jnp.concatenate(imags, 0).astype(BF16)
                return carry

            lax.fori_loop(0, 2, body, 0)

    def product(t, h, left, first=0, count=4):
        cols = slice(2 * LANES * first, 2 * LANES * (first + count))
        bins = slice(2 * LANES * (2 * h + first), 2 * LANES * (2 * h + first + count))
        return jnp.dot(left[h, :, cols], table[t, bins, :], preferred_element_type=F32)

    def r_copy(h):
        return remote(r_out.at[h], r_in.at[:, h], ro_sem.at[h], ri_sem.at[h], sta, beside[1 - h])

    def all_out(u, carry):
        each_start(u, True)
        return carry

    def all_tables(t, carry):
        for n in range(6):
            table_copy(t, n).start()
        return carry

    lax.fori_loop(0, 2 * steps, all_out, 0)
    lax.fori_loop(0, steps, all_tables, 0)
    acc[...] = jnp.zeros_like(acc)
    o_ref[...] = jnp.zeros_like(o_ref)

    def near(t):
        cross(t, OWN, 1, lhs)
        for u in (2 * t, 2 * t + 1):
            arrived(y_buf.at[MATE, u], y_sem.at[MATE, u])
            arrived(x_in.at[MATE, u], x_sem.at[MATE, u])
        cross(t, MATE, 1, lhs)

    def far_mate(t):
        for u in (2 * t, 2 * t + 1):
            arrived(y_buf.at[FARMATE, u], y_sem.at[FARMATE, u])
            arrived(x_far.at[1, u, :, core], x_sem.at[FARMATE, u])
        cross(t, FARMATE, 1, lhs)

    def tables_here(t):
        for n in range(6):
            table_copy(t, n).wait()

    early(0)
    enter(0)
    early(1)
    enter(1)
    second(0)
    early(2)
    near(0)

    def step(t, carry):
        enter(2 * t)
        second(2 * t - 1)
        early(2 * t + 1)
        cross(t - 1, FAR, 1, lhs)
        enter(2 * t + 1)
        far_mate(t - 1)
        tables_here(t - 1)
        for h in range(2):
            acc[h] += product(t - 1, h, lhs)
        second(2 * t)

        @pl.when(t < steps - 1)
        def _():
            early(2 * t + 2)

        near(t)
        return carry

    lax.fori_loop(1, steps, step, 0)

    end = steps - 1
    tables_here(end)
    second(2 * steps - 1)
    cross(end, FAR, 1, lhs)
    for h in range(2):
        acc[h] += product(end, h, lhs, 1 - h, 3)
    far_mate(end)
    for h in range(2):
        r_out[h] = (acc[h] + product(end, h, lhs, 3 * h, 1)).astype(BF16).reshape(8, 32, LAGS)
        r_copy(h).start()

    def mine(t, carry):
        for src in range(4):
            cross(t, src, 0, lhs)
        for h in range(2):
            o_ref[:, h] += product(t, h, lhs).reshape(8, 32, LAGS)
        return carry

    lax.fori_loop(0, steps, mine, 0)

    def drain(u, carry):
        each_start(u, False)

        @pl.when(x_pass)
        def _():
            x_relay(u).wait_send()

        @pl.when(y_pass)
        def _():
            y_relay(u).wait_send()

        for copy in y_sides(u) + [y_mate(u), y_far(u)] + x_sides(u) + [x_mate(u), x_hand(u)]:
            copy.wait_send()
        return carry

    lax.fori_loop(0, 2 * steps, drain, 0)
    for h in range(2):
        r_copy(h).wait()


def finish(norm, own_ref, others_ref, o_ref, buf, sem):
    def out(a):
        return pltpu.make_async_copy(buf.at[a], o_ref.at[a], sem.at[a])

    for a in range(8):
        buf[a] = (own_ref[a] + others_ref[a].astype(F32)) * norm
        out(a).start()
    for a in range(8):
        out(a).wait()


def on_device(rows_z, parts, spectra, pair_blocks):
    del pair_blocks
    bins_local = spectra.shape[3]
    steps = bins_local // LANES
    bins_total = bins_local * parts
    norm = 1.0 / math.sqrt(WIN * bins_total)
    table = jnp.asarray(table_pieces(parts, steps, bins_total))
    rows = lax.optimization_barrier(spectra.reshape(WIN * BLK, 2 * bins_local))
    pieces = rows.reshape(WIN, 8, 8, 2, steps, LANES).transpose(4, 3, 1, 0, 2, 5)
    pieces = pieces.reshape(2 * steps, 8, BLK, LANES)
    dma = pltpu.SemaphoreType.DMA
    own, others = pl.pallas_call(
        functools.partial(kernel, rows_z, steps),
        out_shape=(jax.ShapeDtypeStruct((8, 2, 32, LAGS), F32), jax.ShapeDtypeStruct((8, 2, 32, LAGS), BF16)),
        in_specs=[pl.BlockSpec(memory_space=pl.ANY)] * 2,
        out_specs=(pl.BlockSpec(memory_space=pltpu.VMEM),) * 2,
        scratch_shapes=[
            pltpu.VMEM((4, 2 * steps, 8, BLK, LANES), BF16),
            pltpu.VMEM((2, 2 * steps, 8, BLK, LANES), BF16),
            pltpu.VMEM((2, 2 * steps, 4, 2, BLK, LANES), BF16),
            pltpu.VMEM((steps, 12 * LANES, LAGS), BF16),
            pltpu.VMEM((2, 256, 8 * LANES), BF16),
            pltpu.VMEM((2, 3, BLK, LANES), F32),
            pltpu.VMEM((2, 256, LAGS), F32),
            pltpu.VMEM((2, 8, 32, LAGS), BF16),
            dma((2 * steps,)), dma((2 * steps,)), dma((2 * steps,)), dma((2 * steps,)),
            dma((4, 2 * steps)), dma((4, 2 * steps)), dma((steps, 6)),
            dma((2 * steps,)), dma((2 * steps,)), dma((2 * steps, 4)), dma((2 * steps, 4)),
            dma((2 * steps, 4)), dma((2 * steps, 6)), dma((2,)), dma((2,)),
        ],
        compiler_params=pltpu.CompilerParams(
            collective_id=0, has_side_effects=True, vmem_limit_bytes=44 * 1024 * 1024),
        cost_estimate=pl.CostEstimate(flops=9_000_000_000, bytes_accessed=24_000_000, transcendentals=0),
    )(pieces, table)
    out = pl.pallas_call(
        functools.partial(finish, norm),
        out_shape=jax.ShapeDtypeStruct((8, 2, 32, LAGS), F32),
        in_specs=[pl.BlockSpec(memory_space=pltpu.VMEM)] * 2,
        out_specs=pl.BlockSpec(memory_space=pl.ANY),
        scratch_shapes=[pltpu.VMEM((8, 2, 32, LAGS), F32), dma((8,))],
        compiler_params=pltpu.CompilerParams(vmem_limit_bytes=8 * 1024 * 1024),
    )(own, others)
    return out.reshape(8, 1, BLK, LAGS)


def solution(mesh):
    rows_z = mesh.shape["sta"] // NY
    return jax.shard_map(
        functools.partial(on_device, rows_z, mesh.shape["freq"]),
        mesh=mesh,
        in_specs=(P(None, "sta", None, "freq"), P("sta", None)),
        out_specs=P("freq", "sta", None, None),
        check_vma=False,
    )
```
